512 devices in a mesh: narrow: 16 (over x, y_lo), wide: 32 (over y_hi, z, core).
Axes of the slice: x: 4, y: 8 (y_hi: 2, y_lo: 4; y = y_hi * 4 + y_lo), z: 8, core: 2. Of those that a mesh axis runs over, the one named last changes fastest.
Arguments:
- out_grads: bfloat16 [512, 28672], P('wide', 'narrow'), may hold values from -0.5 to 0.5
- activations: bfloat16 [512, 8192], P('narrow', 'wide'), may hold values from -6 to 6
- grad_basis: bfloat16 [28672, 28672], P('narrow', 'wide'), may hold values from -0.03125 to 0.03125
- act_basis: bfloat16 [8192, 8192], P('wide', 'narrow'), may hold values from -0.0625 to 0.0625
Outputs:
- correction: bfloat16 [8192, 28672], P('narrow', 'wide')
The draws below stay inside these ranges and needn't reach their ends.
All inputs are finite; a program needn't handle non-finite values.
Results may differ from the reference program's by a relative error of at most 0.0058.
Values may be sent and summed in bfloat16 or wider, within the bound.
No kernel may reach another device: no remote copies, remote signals or barrier semaphores. Data moves between devices by JAX's collectives and lax.ppermute only.
A program may use at most 64 MiB of HBM per device.

```python
import jax
import jax.numpy as jnp
from jax import lax

D_IN = 8192
D_OUT = 28672
SEQS = 2
SEQ_LEN = 256
TOKENS = 512


def shard_levels(stream_key, dims, shards, least, top_value):
    level = 1.0
    for position, shards_of in shards:
        steps = jax.random.uniform(jax.random.fold_in(jax.random.fold_in(stream_key, 6), position), (shards_of,), jnp.float32, least / len(shards), top_value / len(shards))
        level = level * jnp.repeat(jnp.exp(steps), dims[position] // shards_of).reshape((-1,) + (1,) * (len(dims) - 1 - position))
    return level


def gaussian(stream_key, shape, scale, bound, split=(), kind=jnp.bfloat16):
    factor_of = shard_levels(stream_key, shape, split, -0.22, 0.18) if split else 1.0
    drawn = jax.random.normal(stream_key, shape, jnp.float32) * scale * factor_of
    return jnp.minimum(jnp.maximum(drawn, -bound), bound).astype(kind)


def setup_inputs(seed: int = 0) -> dict:
    arg_keys = jax.random.split(jax.random.key(seed), 5)
    return {
        "out_grads": gaussian(arg_keys[0], (TOKENS, D_OUT), 0.0625, 0.5, ((0, 32), (1, 16))),
        "activations": gaussian(arg_keys[1], (TOKENS, D_IN), 1.0, 6.0, ((0, 16), (1, 32))),
        "grad_basis": gaussian(arg_keys[2], (D_OUT, D_OUT), D_OUT ** -0.5, 0.03125, ((0, 16), (1, 32))),
        "act_basis": gaussian(arg_keys[3], (D_IN, D_IN), D_IN ** -0.5, 0.0625, ((0, 32), (1, 16))),
    }


def reference(out_grads, activations, grad_basis, act_basis):
    grad_rot = jnp.dot(out_grads, grad_basis, preferred_element_type=jnp.float32).astype(jnp.bfloat16)
    act_rot = jnp.dot(activations, act_basis, preferred_element_type=jnp.float32).astype(jnp.bfloat16)
    grad_seq = grad_rot.reshape(SEQS, SEQ_LEN, D_OUT).astype(jnp.float32)
    width = 256 if D_IN % 256 == 0 else D_IN
    act_blocks = act_rot.reshape(SEQS, SEQ_LEN, D_IN // width, width).transpose(2, 0, 1, 3).astype(jnp.float32)

    def one_block(block):
        products = jnp.einsum("sti,stj->sij", block, grad_seq)
        return jnp.mean(products * products, axis=0).astype(jnp.bfloat16)

    result = lax.map(one_block, act_blocks)
    return result.reshape(D_IN, D_OUT)
```

```python
import jax
import jax.numpy as jnp
from jax import lax
from jax.experimental import pallas as pl
from jax.experimental.pallas import tpu as pltpu
from jax.sharding import Mesh, PartitionSpec as P

F32 = jnp.float32
BF16 = jnp.bfloat16
SEQS = 2
NARROW = ("x", "y_lo")
PLANE = ("y_hi", "z")
WIDE = PLANE + ("core",)
SIZES = (4, 4, 2, 8, 2)
PAIR = [(0, 1), (1, 0)]
VMEM = 40 * 2**20


def call(body, outs, *args, flops=0):
    moved = sum(a.size * a.dtype.itemsize for a in args)
    return pl.pallas_call(
        body,
        out_shape=outs,
        compiler_params=pltpu.CompilerParams(vmem_limit_bytes=VMEM),
        cost_estimate=pl.CostEstimate(flops=flops, bytes_accessed=moved, transcendentals=0),
    )(*args)


def spread(copies, axes):
    return lax.all_to_all(copies, axes, 0, 0)


def act_product(acts_ref, basis_ref, keep_ref, send_ref):
    core = lax.axis_index("core")
    for ref, part in ((keep_ref, core), (send_ref, 1 - core)):
        rows = acts_ref[:, pl.ds(part, 1)]
        rows = rows.reshape(ref.shape[0], basis_ref.shape[0])
        ref[...] = jnp.dot(rows, basis_ref[...], preferred_element_type=F32)


def add_pair(keep_ref, recv_ref, out_ref):
    out_ref[...] = (keep_ref[...] + recv_ref[...]).astype(BF16).reshape(out_ref.shape)


def add_and_copy(parts_ref, out_ref):
    total = parts_ref[0].astype(F32)
    for i in range(1, parts_ref.shape[0]):
        total = total + parts_ref[i].astype(F32)
    total = total.astype(BF16)
    for i in range(out_ref.shape[0]):
        out_ref[i] = total


def grad_product(own_ref, other_ref, basis_ref, out_ref):
    count, _, rows, width = out_ref.shape
    for which, ref in enumerate((own_ref, other_ref)):
        block = ref[...].reshape(count * rows, basis_ref.shape[0])
        part = jnp.dot(block, basis_ref[...], preferred_element_type=F32)
        out_ref[:, which] = part.astype(BF16).reshape(count, rows, width)


def correct(own_ref, other_ref, grad_ref, out_ref):
    count = grad_ref.shape[0] // SEQS
    total = None
    for seq in range(SEQS):
        part = slice(seq * count, (seq + 1) * count)
        acts = jnp.stack([own_ref[part], other_ref[part]], axis=1)
        acts = acts.reshape(-1, acts.shape[-1])
        grads = grad_ref[part].reshape(-1, grad_ref.shape[-1])
        product = lax.dot_general(acts, grads, (((0,), (0,)), ((), ())), preferred_element_type=F32)
        square = product * product
        total = square if total is None else total + square
    out_ref[...] = (total * (1.0 / SEQS)).astype(BF16)


def shards(out_grads, activations, grad_basis, act_basis):
    rows, depth = out_grads.shape
    acts_in = activations.shape[1]
    acts_out = act_basis.shape[1]
    width = grad_basis.shape[1]
    shape = jax.ShapeDtypeStruct

    grads = spread(jnp.broadcast_to(out_grads, (16, rows, depth)), PLANE)
    grads_other = lax.ppermute(grads, "core", PAIR)

    acts = activations.reshape(1, 2, rows, acts_in)
    acts = spread(jnp.broadcast_to(acts, (16, 2, rows, acts_in)), NARROW)
    half = shape((16 * rows, acts_out), F32)
    keep, send = call(act_product, (half, half), acts, act_basis)
    recv = lax.ppermute(send, "core", PAIR)
    act_half = call(add_pair, shape((16, rows, acts_out), BF16), keep, recv)
    act_parts = spread(act_half, PLANE)
    act_rot = call(add_and_copy, shape((16, rows, acts_out), BF16), act_parts)
    act_own = spread(act_rot, PLANE)
    act_other = lax.ppermute(act_own, "core", PAIR)

    grad_part = call(grad_product, shape((16, 2, rows, width), BF16), grads, grads_other, grad_basis)
    grad_parts = spread(grad_part, NARROW)
    grad_rot = call(add_and_copy, shape((4, 2, rows, width), BF16), grad_parts)
    grad_rot = spread(grad_rot, "y_lo")
    grad_rot = lax.all_gather(grad_rot, "x", axis=0, tiled=True)

    return call(correct, shape((acts_out, width), BF16), act_own, act_other, grad_rot)


def solution(mesh):
    fine = Mesh(mesh.devices.reshape(SIZES), NARROW + WIDE)
    return jax.shard_map(
        shards,
        mesh=fine,
        in_specs=(
            P(WIDE, NARROW),
            P(NARROW, WIDE),
            P(NARROW, WIDE),
            P(WIDE, NARROW),
        ),
        out_specs=P(NARROW, WIDE),
        check_vma=False,
    )
```

```python
import jax
import jax.numpy as jnp
from jax import lax
from jax.experimental import pallas as pl
from jax.experimental.pallas import tpu as pltpu
from jax.sharding import Mesh, PartitionSpec as P

F32 = jnp.float32
BF16 = jnp.bfloat16
SEQS = 2
NARROW = ("x", "y_lo")
PLANE = ("y_hi", "z")
WIDE = PLANE + ("core",)
SIZES = (4, 4, 2, 8, 2)
PAIR = [(0, 1), (1, 0)]
VMEM = 40 * 2**20
STEP = 896
shape = jax.ShapeDtypeStruct


def call(body, outs, *args, flops=0, **more):
    moved = sum(a.size * a.dtype.itemsize for a in args)
    return pl.pallas_call(
        body,
        out_shape=outs,
        compiler_params=pltpu.CompilerParams(vmem_limit_bytes=VMEM),
        cost_estimate=pl.CostEstimate(flops=flops, bytes_accessed=moved, transcendentals=0),
        **more,
    )(*args)


def spread(copies, axes):
    return lax.all_to_all(copies, axes, 0, 0)


def act_product(acts_ref, basis_ref, keep_ref, send_ref):
    core = lax.axis_index("core")
    for ref, part in ((keep_ref, core), (send_ref, 1 - core)):
        rows = acts_ref[:, pl.ds(part, 1)]
        rows = rows.reshape(ref.shape[0], basis_ref.shape[0])
        ref[...] = jnp.dot(rows, basis_ref[...], preferred_element_type=F32)


def pack(grads_ref, keep_ref, recv_ref, out_ref):
    count = out_ref.shape[0]
    half, rows, depth = grads_ref.shape
    for i in range(count):
        for j in range(half):
            part = slice((j * count + i) * rows, (j * count + i + 1) * rows)
            out_ref[i, j, :, :depth] = grads_ref[j]
            out_ref[i, j, :, depth:] = (keep_ref[part] + recv_ref[part]).astype(BF16)


def total_of(parts):
    total = parts[0].astype(F32)
    for i in range(1, parts.shape[0]):
        total = total + parts[i].astype(F32)
    return total


def add_acts(packed_ref, out_ref):
    out_ref[...] = total_of(packed_ref[:, :, :, packed_ref.shape[3] - out_ref.shape[2]:])


def add_far(own_ref, far_ref, out_ref):
    out_ref[...] = (own_ref[...] + far_ref[...]).astype(BF16)


def place(own_ref, other_ref, out_ref):
    here = lax.axis_index("y_hi")
    out_ref[pl.ds(here, 1)] = own_ref[...][None]
    out_ref[pl.ds(1 - here, 1)] = other_ref[...][None]


def add_grads(parts_ref, out_ref):
    total = total_of(parts_ref).astype(BF16)
    for i in range(out_ref.shape[0]):
        out_ref[i] = total


def own_product(own_ref, basis_ref, out_ref, sums_ref):
    step = pl.program_id(0)
    block = own_ref[...].reshape(sums_ref.shape[0], STEP)
    part = jnp.dot(block, basis_ref[...], preferred_element_type=F32)

    @pl.when(step == 0)
    def _():
        sums_ref[...] = part

    @pl.when(step == pl.num_programs(0) - 1)
    def _():
        out_ref[...] = (sums_ref[...] + part).astype(BF16)


def other_product(first_ref, other_ref, basis_ref, out_ref, sums_ref):
    step = pl.program_id(0)
    halves, count, _, rows, width = out_ref.shape
    block = other_ref[...].reshape(sums_ref.shape[0], STEP)
    part = jnp.dot(block, basis_ref[...], preferred_element_type=F32)

    @pl.when(step == 0)
    def _():
        sums_ref[...] = part
        first = first_ref[...].reshape(count, halves, rows, width)
        for j in range(halves):
            out_ref[j, :, 0] = first[:, j]

    @pl.when(step == pl.num_programs(0) - 1)
    def _():
        last = (sums_ref[...] + part).astype(BF16).reshape(count, halves, rows, width)
        for j in range(halves):
            out_ref[j, :, 1] = last[:, j]


def correct(own_ref, other_ref, grad_ref, out_ref):
    count = grad_ref.shape[0] // SEQS
    total = None
    for seq in range(SEQS):
        acts = jnp.stack([own_ref[:, seq], other_ref[:, seq]], axis=1)
        acts = acts.reshape(-1, acts.shape[-1])
        grads = grad_ref[seq * count:(seq + 1) * count]
        grads = grads.reshape(-1, grads.shape[-1])
        product = lax.dot_general(acts, grads, (((0,), (0,)), ((), ())), preferred_element_type=F32)
        square = product * product
        total = square if total is None else total + square
    out_ref[...] = (total * (1.0 / SEQS)).astype(BF16)


def shards(out_grads, activations, grad_basis, act_basis):
    rows, depth = out_grads.shape
    acts_in = activations.shape[1]
    acts_out = act_basis.shape[1]
    width = grad_basis.shape[1]

    acts = activations.reshape(1, 2, rows, acts_in)
    acts = spread(jnp.broadcast_to(acts, (16, 2, rows, acts_in)), NARROW)
    grads_far = lax.ppermute(out_grads, "y_hi", PAIR)
    grads = call(place, shape((2, rows, depth), BF16), out_grads, grads_far)
    acts, grads = lax.optimization_barrier((acts, grads))
    half = shape((16 * rows, acts_out), F32)
    keep, send = call(act_product, (half, half), acts, act_basis)
    recv = lax.ppermute(send, "core", PAIR)

    packed = call(pack, shape((8, 2, rows, depth + acts_out), BF16), grads, keep, recv)
    packed = spread(packed, "z")
    packed_other = lax.ppermute(packed, "core", PAIR)

    act_near = call(add_acts, shape((2, rows, acts_out), F32), packed)
    act_far = lax.ppermute(act_near, "y_hi", PAIR)

    specs = [
        pl.BlockSpec((8, 2, rows, STEP), lambda k: (0, 0, 0, k)),
        pl.BlockSpec((STEP, width), lambda k: (k, 0)),
    ]
    more = dict(grid=(depth // STEP,), scratch_shapes=[pltpu.VMEM((16 * rows, width), F32)])
    first = call(
        own_product,
        shape((16 * rows, width), BF16),
        packed,
        grad_basis,
        in_specs=specs,
        out_specs=pl.BlockSpec((16 * rows, width), lambda k: (0, 0)),
        **more,
    )
    grad_part = call(
        other_product,
        shape((2, 8, 2, rows, width), BF16),
        first,
        packed_other,
        grad_basis,
        in_specs=[pl.BlockSpec((16 * rows, width), lambda k: (0, 0))] + specs,
        out_specs=pl.BlockSpec((2, 8, 2, rows, width), lambda k: (0, 0, 0, 0, 0)),
        **more,
    )
    act_two = call(add_far, shape((2, rows, acts_out), BF16), act_near, act_far)
    grad_part, act_two = lax.optimization_barrier((grad_part, act_two))
    grad_parts = spread(grad_part.reshape(16, 2, rows, width), NARROW)
    act_own = lax.all_gather(act_two, "z", axis=0)
    grad_parts, act_own = lax.optimization_barrier((grad_parts, act_own))
    act_other = lax.ppermute(act_own, "core", PAIR)

    grad_rot = call(add_grads, shape((4, 2, rows, width), BF16), grad_parts)
    grad_rot = spread(grad_rot, "y_lo")
    grad_rot = lax.all_gather(grad_rot, "x", axis=0, tiled=True)
    return call(correct, shape((acts_out, width), BF16), act_own, act_other, grad_rot)


def solution(mesh):
    fine = Mesh(mesh.devices.reshape(SIZES), NARROW + WIDE)
    return jax.shard_map(
        shards,
        mesh=fine,
        in_specs=(
            P(WIDE, NARROW),
            P(NARROW, WIDE),
            P(NARROW, WIDE),
            P(WIDE, NARROW),
        ),
        out_specs=P(NARROW, WIDE),
        check_vma=False,
    )
```

```python
import jax
import jax.numpy as jnp
from jax import lax
from jax.experimental import pallas as pl
from jax.experimental.pallas import tpu as pltpu
from jax.sharding import Mesh, PartitionSpec as P

F32 = jnp.float32
BF16 = jnp.bfloat16
SEQS = 2
NARROW = ("x", "y_lo")
PLANE = ("y_hi", "z")
WIDE = PLANE + ("core",)
SIZES = (4, 4, 2, 8, 2)
PAIR = [(0, 1), (1, 0)]
VMEM = 40 * 2**20
STEP = 896
shape = jax.ShapeDtypeStruct


def call(body, outs, *args, flops=0, **more):
    moved = sum(a.size * a.dtype.itemsize for a in args)
    return pl.pallas_call(
        body,
        out_shape=outs,
        compiler_params=pltpu.CompilerParams(vmem_limit_bytes=VMEM),
        cost_estimate=pl.CostEstimate(flops=flops, bytes_accessed=moved, transcendentals=0),
        **more,
    )(*args)


def spread(copies, axes):
    return lax.all_to_all(copies, axes, 0, 0)


def act_product(acts_ref, basis_ref, keep_ref, send_ref):
    core = lax.axis_index("core")
    for ref, part in ((keep_ref, core), (send_ref, 1 - core)):
        rows = acts_ref[:, pl.ds(part, 1)]
        rows = rows.reshape(ref.shape[0], basis_ref.shape[0])
        ref[...] = jnp.dot(rows, basis_ref[...], preferred_element_type=F32)


def pack(grads_ref, keep_ref, recv_ref, out_ref):
    count, rows, _ = out_ref.shape
    depth = grads_ref.shape[1]
    for i in range(count):
        part = slice(i * rows, (i + 1) * rows)
        out_ref[i, :, :depth] = grads_ref[...]
        out_ref[i, :, depth:] = (keep_ref[part] + recv_ref[part]).astype(BF16)


def total_of(parts):
    total = parts[0].astype(F32)
    for i in range(1, parts.shape[0]):
        total = total + parts[i].astype(F32)
    return total


def add_acts(packed_ref, out_ref):
    out_ref[...] = total_of(packed_ref[:, :, packed_ref.shape[2] - out_ref.shape[1]:]).astype(BF16)


def add_grads(parts_ref, out_ref):
    total = total_of(parts_ref).astype(BF16)
    for i in range(out_ref.shape[0]):
        out_ref[i] = total


def own_product(own_ref, basis_ref, out_ref, sums_ref):
    step = pl.program_id(0)
    block = own_ref[...].reshape(sums_ref.shape[0], STEP)
    part = jnp.dot(block, basis_ref[...], preferred_element_type=F32)

    @pl.when(step == 0)
    def _():
        sums_ref[...] = part

    @pl.when(step == pl.num_programs(0) - 1)
    def _():
        out_ref[...] = (sums_ref[...] + part).astype(BF16)


def other_product(first_ref, other_ref, basis_ref, out_ref, sums_ref):
    step = pl.program_id(0)
    core = lax.axis_index("core")
    count, _, rows, width = out_ref.shape
    block = other_ref[...].reshape(sums_ref.shape[0], STEP)
    part = jnp.dot(block, basis_ref[...], preferred_element_type=F32)

    @pl.when(step == 0)
    def _():
        sums_ref[...] = part
        out_ref[:, pl.ds(core, 1)] = first_ref[...].reshape(count, 1, rows, width)

    @pl.when(step == pl.num_programs(0) - 1)
    def _():
        last = (sums_ref[...] + part).astype(BF16)
        out_ref[:, pl.ds(1 - core, 1)] = last.reshape(count, 1, rows, width)


def correct(near_ref, far_ref, grad_ref, out_ref):
    count = grad_ref.shape[0] // SEQS
    seq = lax.axis_index("y_hi")
    total = None
    for which, ref in ((seq, near_ref), (1 - seq, far_ref)):
        acts = jnp.stack([ref[0], ref[1]], axis=1)
        acts = acts.reshape(-1, acts.shape[-1])
        grads = grad_ref[pl.ds(which * count, count)]
        grads = grads.reshape(-1, grads.shape[-1])
        product = lax.dot_general(acts, grads, (((0,), (0,)), ((), ())), preferred_element_type=F32)
        square = product * product
        total = square if total is None else total + square
    out_ref[...] = (total * (1.0 / SEQS)).astype(BF16)


def shards(out_grads, activations, grad_basis, act_basis):
    rows, depth = out_grads.shape
    acts_in = activations.shape[1]
    acts_out = act_basis.shape[1]
    width = grad_basis.shape[1]

    acts = activations.reshape(1, 2, rows, acts_in)
    acts = spread(jnp.broadcast_to(acts, (16, 2, rows, acts_in)), NARROW)
    half = shape((16 * rows, acts_out), F32)
    keep, send = call(act_product, (half, half), acts, act_basis)
    recv = lax.ppermute(send, "core", PAIR)

    packed = call(pack, shape((16, rows, depth + acts_out), BF16), out_grads, keep, recv)
    packed = spread(packed, PLANE)
    packed_other = lax.ppermute(packed, "core", PAIR)
    act_rot = call(add_acts, shape((rows, acts_out), BF16), packed)

    specs = [
        pl.BlockSpec((16, rows, STEP), lambda k: (0, 0, k)),
        pl.BlockSpec((STEP, width), lambda k: (k, 0)),
    ]
    more = dict(grid=(depth // STEP,), scratch_shapes=[pltpu.VMEM((16 * rows, width), F32)])
    first = call(
        own_product,
        shape((16 * rows, width), BF16),
        packed,
        grad_basis,
        in_specs=specs,
        out_specs=pl.BlockSpec((16 * rows, width), lambda k: (0, 0)),
        **more,
    )
    grad_part = call(
        other_product,
        shape((16, 2, rows, width), BF16),
        first,
        packed_other,
        grad_basis,
        in_specs=[pl.BlockSpec((16 * rows, width), lambda k: (0, 0))] + specs,
        out_specs=pl.BlockSpec((16, 2, rows, width), lambda k: (0, 0, 0, 0)),
        **more,
    )
    grad_part, act_rot = lax.optimization_barrier((grad_part, act_rot))
    grad_parts = spread(grad_part, NARROW)
    act_near = lax.all_gather(act_rot, "z", axis=0)
    grad_parts, act_near = lax.optimization_barrier((grad_parts, act_near))

    grad_rot = call(add_grads, shape((4, 2, rows, width), BF16), grad_parts)
    grad_rot = spread(grad_rot, "y_lo")
    act_near = lax.all_gather(act_near, "core", axis=0)
    act_far = lax.ppermute(act_near, "y_hi", PAIR)
    grad_rot, act_near = lax.optimization_barrier((grad_rot, act_near))
    grad_rot = lax.all_gather(grad_rot, "x", axis=0, tiled=True)
    return call(correct, shape((acts_out, width), BF16), act_near, act_far, grad_rot)


def solution(mesh):
    fine = Mesh(mesh.devices.reshape(SIZES), NARROW + WIDE)
    return jax.shard_map(
        shards,
        mesh=fine,
        in_specs=(
            P(WIDE, NARROW),
            P(NARROW, WIDE),
            P(NARROW, WIDE),
            P(WIDE, NARROW),
        ),
        out_specs=P(NARROW, WIDE),
        check_vma=False,
    )
```

```python
import functools

import jax
import jax.numpy as jnp
from jax import lax
from jax.experimental import pallas as pl
from jax.experimental.pallas import tpu as pltpu
from jax.sharding import Mesh, PartitionSpec as P

F32 = jnp.float32
BF16 = jnp.bfloat16
SEQS = 2
NARROW = ("x", "y_lo")
PLANE = ("y_hi", "z")
WIDE = PLANE + ("core",)
SIZES = (4, 4, 2, 8, 2)
PAIR = [(0, 1), (1, 0)]
VMEM = 40 * 2**20
STEP = 896
shape = jax.ShapeDtypeStruct


def call(body, outs, *args, flops=0, **more):
    moved = sum(a.size * a.dtype.itemsize for a in args)
    return pl.pallas_call(
        body,
        out_shape=outs,
        compiler_params=pltpu.CompilerParams(vmem_limit_bytes=VMEM),
        cost_estimate=pl.CostEstimate(flops=flops, bytes_accessed=moved, transcendentals=0),
        **more,
    )(*args)


def spread(copies, axes):
    return lax.all_to_all(copies, axes, 0, 0)


def act_product(flip, acts_ref, basis_ref, out_ref):
    core = lax.axis_index("core")
    rows = acts_ref[:, pl.ds(1 - core if flip else core, 1)]
    rows = rows.reshape(out_ref.shape[0], basis_ref.shape[0])
    out_ref[...] = jnp.dot(rows, basis_ref[...], preferred_element_type=F32)


def pack(grads_ref, keep_ref, recv_ref, out_ref):
    count, rows, _ = out_ref.shape
    depth = grads_ref.shape[1]
    for i in range(count):
        part = slice(i * rows, (i + 1) * rows)
        out_ref[i, :, :depth] = grads_ref[...]
        out_ref[i, :, depth:] = (keep_ref[part] + recv_ref[part]).astype(BF16)


def total_of(parts):
    total = parts[0].astype(F32)
    for i in range(1, parts.shape[0]):
        total = total + parts[i].astype(F32)
    return total


def add_acts(packed_ref, out_ref):
    out_ref[...] = total_of(packed_ref[:, :, packed_ref.shape[2] - out_ref.shape[1]:]).astype(BF16)


def add_grads(parts_ref, out_ref):
    total = total_of(parts_ref).astype(BF16)
    for i in range(out_ref.shape[0]):
        out_ref[i] = total


def own_product(own_ref, basis_ref, out_ref, sums_ref):
    step = pl.program_id(0)
    block = own_ref[...].reshape(sums_ref.shape[0], STEP)
    part = jnp.dot(block, basis_ref[...], preferred_element_type=F32)

    @pl.when(step == 0)
    def _():
        sums_ref[...] = part

    @pl.when(step == pl.num_programs(0) - 1)
    def _():
        out_ref[...] = (sums_ref[...] + part).astype(BF16)


def other_product(first_ref, other_ref, basis_ref, out_ref, sums_ref):
    step = pl.program_id(0)
    core = lax.axis_index("core")
    count, _, rows, width = out_ref.shape
    block = other_ref[...].reshape(sums_ref.shape[0], STEP)
    part = jnp.dot(block, basis_ref[...], preferred_element_type=F32)

    @pl.when(step == 0)
    def _():
        sums_ref[...] = part
        out_ref[:, pl.ds(core, 1)] = first_ref[...].reshape(count, 1, rows, width)

    @pl.when(step == pl.num_programs(0) - 1)
    def _():
        last = (sums_ref[...] + part).astype(BF16)
        out_ref[:, pl.ds(1 - core, 1)] = last.reshape(count, 1, rows, width)


def correct(near_ref, far_ref, grad_ref, out_ref):
    count = grad_ref.shape[0] // SEQS
    seq = lax.axis_index("y_hi")
    total = None
    for which, ref in ((seq, near_ref), (1 - seq, far_ref)):
        acts = jnp.stack([ref[0], ref[1]], axis=1)
        acts = acts.reshape(-1, acts.shape[-1])
        grads = grad_ref[pl.ds(which * count, count)]
        grads = grads.reshape(-1, grads.shape[-1])
        product = lax.dot_general(acts, grads, (((0,), (0,)), ((), ())), preferred_element_type=F32)
        square = product * product
        total = square if total is None else total + square
    out_ref[...] = (total * (1.0 / SEQS)).astype(BF16)


def shards(out_grads, activations, grad_basis, act_basis):
    rows, depth = out_grads.shape
    acts_in = activations.shape[1]
    acts_out = act_basis.shape[1]
    width = grad_basis.shape[1]

    acts = activations.reshape(1, 2, rows, acts_in)
    acts = spread(jnp.broadcast_to(acts, (16, 2, rows, acts_in)), NARROW)
    half = shape((16 * rows, acts_out), F32)
    send = call(functools.partial(act_product, True), half, acts, act_basis)
    recv = lax.ppermute(send, "core", PAIR)
    keep = call(functools.partial(act_product, False), half, acts, act_basis)

    packed = call(pack, shape((16, rows, depth + acts_out), BF16), out_grads, keep, recv)
    packed = spread(packed, PLANE)
    packed_other = lax.ppermute(packed, "core", PAIR)
    act_rot = call(add_acts, shape((rows, acts_out), BF16), packed)

    specs = [
        pl.BlockSpec((16, rows, STEP), lambda k: (0, 0, k)),
        pl.BlockSpec((STEP, width), lambda k: (k, 0)),
    ]
    more = dict(grid=(depth // STEP,), scratch_shapes=[pltpu.VMEM((16 * rows, width), F32)])
    first = call(
        own_product,
        shape((16 * rows, width), BF16),
        packed,
        grad_basis,
        in_specs=specs,
        out_specs=pl.BlockSpec((16 * rows, width), lambda k: (0, 0)),
        **more,
    )
    grad_part = call(
        other_product,
        shape((16, 2, rows, width), BF16),
        first,
        packed_other,
        grad_basis,
        in_specs=[pl.BlockSpec((16 * rows, width), lambda k: (0, 0))] + specs,
        out_specs=pl.BlockSpec((16, 2, rows, width), lambda k: (0, 0, 0, 0)),
        **more,
    )
    grad_part, act_rot = lax.optimization_barrier((grad_part, act_rot))
    grad_parts = spread(grad_part, NARROW)
    act_near = lax.all_gather(act_rot, "z", axis=0)
    grad_parts, act_near = lax.optimization_barrier((grad_parts, act_near))

    grad_rot = call(add_grads, shape((4, 2, rows, width), BF16), grad_parts)
    grad_rot = spread(grad_rot, "y_lo")
    act_near = lax.all_gather(act_near, "core", axis=0)
    act_far = lax.ppermute(act_near, "y_hi", PAIR)
    grad_rot, act_near = lax.optimization_barrier((grad_rot, act_near))
    grad_rot = lax.all_gather(grad_rot, "x", axis=0, tiled=True)
    act_spec = pl.BlockSpec((2, 8, rows, acts_out // 2), lambda k: (0, 0, 0, k))
    return call(
        correct,
        shape((acts_out, width), BF16),
        act_near,
        act_far,
        grad_rot,
        grid=(2,),
        in_specs=[act_spec, act_spec, pl.BlockSpec((16, 2, rows, width), lambda k: (0, 0, 0, 0))],
        out_specs=pl.BlockSpec((acts_out // 2, width), lambda k: (k, 0)),
    )


def solution(mesh):
    fine = Mesh(mesh.devices.reshape(SIZES), NARROW + WIDE)
    return jax.shard_map(
        shards,
        mesh=fine,
        in_specs=(
            P(WIDE, NARROW),
            P(NARROW, WIDE),
            P(NARROW, WIDE),
            P(WIDE, NARROW),
        ),
        out_specs=P(NARROW, WIDE),
        check_vma=False,
    )
```
